512 devices in a mesh: sample: 64 (over z, x, core), basis: 8 (over y).
Axes of the slice: x: 4, y: 8, z: 8, core: 2. Of those that a mesh axis runs over, the one named last changes fastest.
Arguments:
- points: float32 [10, 131072], P(None, 'sample'), may hold values from -1 to 1
- run_weights: float32 [131072], P('sample'), may hold values from 0.25 to 6.1
- panel_degrees: int32 [10, 128], P(None, 'basis'), may hold values from 0 to 6, as said below
- trailing_degrees: int32 [10, 2048], P(None, 'basis'), may hold values from 0 to 6, as said below
Outputs:
- r_factor: float32 [128, 128], replicated
- coupling: float32 [128, 2048], P(None, 'basis')
- updated: float32 [131072, 2048], P('sample', 'basis')
The draws below stay inside these ranges and needn't reach their ends.
Inputs may be any that keep to these rules, and one draw needn't show every extreme that they name: `panel_degrees`: every column is a multi-index of total degree at most 6; all 2176 columns are distinct. `trailing_degrees`: as for panel_degrees; no trailing column repeats a panel column.
All inputs are finite; a program needn't handle non-finite values.
Results may differ from the reference program's by a relative error of at most 0.0003.
Values sent between devices are 32-bit elements; how exact they have to be, the bound alone decides.
A program may use at most 64 MiB of HBM per device.

```python
import math
import jax
import jax.numpy as jnp
import numpy as np
from jax import lax

DIMS = 10
DEG = 6
PANEL = 128
TRAIL_DEV = 256
RUNS = 131072
TRAIL = 2048
N_BASIS = 8


def multi_indices(dims, top):
    if dims == 1:
        return [[degree] for degree in range(top + 1)]
    result = []
    for degree in range(top + 1):
        for tail in multi_indices(dims - 1, top - degree):
            result.append([degree] + tail)
    return result


def chosen_columns(key):
    listed = multi_indices(DIMS, DEG)
    table = jnp.asarray(np.array(listed, dtype=np.int32))
    count = len(listed)
    first_pure = [DEG] + [0] * (DIMS - 1)
    second_pure = [0, DEG] + [0] * (DIMS - 2)
    first_row = listed.index(first_pure)
    second_row = listed.index(second_pure)
    marked = np.zeros(count, dtype=np.int32)
    marked[first_row] = 1
    marked[second_row] = 1
    marked = jnp.asarray(marked)
    order = jax.random.permutation(jax.random.fold_in(key, 7), count).astype(jnp.int32)
    keys = marked[order] * count + jnp.arange(count, dtype=jnp.int32)
    others = order[jnp.argsort(keys, stable=True)][:count - 2]
    first_index = jnp.array([first_row], dtype=jnp.int32)
    second_index = jnp.array([second_row], dtype=jnp.int32)
    final_order = jnp.concatenate([first_index, others[:PANEL - 1], second_index, others[PANEL - 1:]])
    return table[final_order]


def draw_panel_degrees(key, part):
    return chosen_columns(key)[:PANEL].T


def draw_trailing_degrees(key, part):
    return chosen_columns(key)[PANEL:PANEL + TRAIL].T


def draw_points(key, part):
    return jnp.tanh(jax.random.normal(key, (DIMS, RUNS), jnp.float32))


def draw_run_weights(key, part):
    position = jnp.arange(RUNS, dtype=jnp.float32) / RUNS
    rising = 1.0 + 2.0 * position
    base = jnp.exp(jax.random.uniform(key, (RUNS,), jnp.float32, -0.7, 0.7))
    return base * rising


def setup_inputs(seed: int = 0) -> dict:
    key_list = jax.random.split(jax.random.key(seed), 5)
    points = draw_points(jax.random.fold_in(key_list[4], 71), 0)
    run_weights = draw_run_weights(jax.random.fold_in(key_list[4], 71), 0)
    panel_degrees = draw_panel_degrees(jax.random.fold_in(key_list[4], 71), 0)
    trailing_degrees = draw_trailing_degrees(jax.random.fold_in(key_list[4], 71), 0)
    return dict(points=points, run_weights=run_weights, panel_degrees=panel_degrees, trailing_degrees=trailing_degrees)


def legendre_rows(coord):
    values = [jnp.ones_like(coord), coord]
    for degree in range(1, DEG):
        values.append(((2.0 * degree + 1.0) * coord * values[degree] - degree * values[degree - 1]) / (degree + 1.0))
    return jnp.stack([values[degree] * math.sqrt(2.0 * degree + 1.0) for degree in range(DEG + 1)], axis=0)

def weighted_columns(points, degrees, weights, run_total):
    levels = jnp.arange(DEG + 1, dtype=jnp.int32)
    product = jnp.broadcast_to(jnp.sqrt(weights / run_total)[:, None], (weights.shape[0], degrees.shape[1]))
    for dim_index in range(points.shape[0]):
        table = legendre_rows(points[dim_index])
        selector = (degrees[dim_index][None, :] == levels[:, None]).astype(points.dtype)
        product = product * lax.dot_general(table, selector, (((0,), (0,)), ((), ())), precision=lax.Precision.HIGHEST)
    return product

def reference(points, run_weights, panel_degrees, trailing_degrees):
    panel = weighted_columns(points, panel_degrees, run_weights, float(RUNS))
    ortho, upper = jnp.linalg.qr(panel)
    signs = jnp.where(jnp.diagonal(upper) < 0, -1.0, 1.0).astype(upper.dtype)
    upper = upper * signs[:, None]
    ortho = ortho * signs[None, :]
    blocks = trailing_degrees.reshape(DIMS, N_BASIS, TRAIL_DEV).transpose(1, 0, 2)

    def one_block(block_degrees):
        columns = weighted_columns(points, block_degrees, run_weights, float(RUNS))
        part_coupling = lax.dot_general(ortho, columns, (((0,), (0,)), ((), ())), precision=lax.Precision.HIGHEST)
        part_update = (columns - jnp.dot(ortho, part_coupling, precision=lax.Precision.HIGHEST)) * math.sqrt(RUNS)
        return (part_coupling, part_update)
    couplings, updates = lax.map(one_block, blocks)
    coupling = couplings.transpose(1, 0, 2).reshape(PANEL, TRAIL)
    updated = updates.transpose(1, 0, 2).reshape(RUNS, TRAIL)
    return (upper, coupling, updated)
```

```python
import functools
import math

import jax
import jax.numpy as jnp
from jax import lax
from jax.experimental import pallas as pl
from jax.experimental.pallas import tpu as pltpu
from jax.sharding import PartitionSpec as P

DEG = 6
LEVELS = DEG + 1
TILES = 16
PANEL = 128
TRAIL = 256
COLS = PANEL + TRAIL
RING = 8
MESH = pl.DeviceIdType.MESH
HIGHEST = lax.Precision.HIGHEST
NT = (((1,), (1,)), ((), ()))
TN = (((0,), (0,)), ((), ()))


def dot(left, right, dims):
    return lax.dot_general(left, right, dims, precision=HIGHEST, preferred_element_type=jnp.float32)


def lane_splat(row, lane):
    return jnp.broadcast_to(row[:, lane:lane + 1], (8, 128))


def sublane_splat(row, sublane):
    return jnp.broadcast_to(row[sublane:sublane + 1, :], (8, 128))


def cholesky(gram_ref, upper_ref, inverse_ref):
    sub = lax.broadcasted_iota(jnp.int32, (8, 128), 0)
    lane = lax.broadcasted_iota(jnp.int32, (8, 128), 1)
    gram = [gram_ref[8 * i:8 * i + 8, :] for i in range(16)]
    ident = [jnp.where(lane == sub + 8 * i, 1.0, 0.0) for i in range(16)]
    for k in range(16):
        splats = [lane_splat(gram[k], 8 * k + j) for j in range(8)]
        diag = [[sublane_splat(splats[j], i) if i >= j else None for j in range(8)] for i in range(8)]
        low = [[None] * 8 for _ in range(8)]
        inv = [None] * 8
        for j in range(8):
            inv[j] = lax.rsqrt(diag[j][j])
            for i in range(j + 1, 8):
                low[i][j] = diag[i][j] * inv[j]
            for i in range(j + 1, 8):
                for m in range(i, 8):
                    diag[m][i] = diag[m][i] - low[m][j] * low[i][j]
        up, lo = [], []
        for j in range(8):
            a, b = sublane_splat(gram[k], j), sublane_splat(ident[k], j)
            for i in range(j):
                a = a - low[j][i] * up[i]
                b = b - low[j][i] * lo[i]
            up.append(a * inv[j])
            lo.append(b * inv[j])
        up_rows, lo_rows = up[0], lo[0]
        for j in range(1, 8):
            up_rows = jnp.where(sub == j, up[j], up_rows)
            lo_rows = jnp.where(sub == j, lo[j], lo_rows)
        upper_ref[8 * k:8 * k + 8, :] = jnp.where(lane >= sub + 8 * k, up_rows, 0.0)
        inverse_ref[8 * k:8 * k + 8, :] = lo_rows
        if k == 15:
            break
        for j in reversed(range(8)):
            for i in range(j + 1, 8):
                up[j] = up[j] - low[i][j] * up[i]
                lo[j] = lo[j] - low[i][j] * lo[i]
            up[j] = up[j] * inv[j]
            lo[j] = lo[j] * inv[j]
        for i in range(k + 1, 16):
            for j in range(8):
                c = lane_splat(gram[i], 8 * k + j)
                if j == 0:
                    a, b = c * up[0], c * lo[0]
                else:
                    a, b = a + c * up[j], b + c * lo[j]
            gram[i] = gram[i] - a
            ident[i] = ident[i] - b


def legendre(coord):
    values = [jnp.ones_like(coord), coord]
    for k in range(1, DEG):
        values.append(((2.0 * k + 1.0) * coord * values[k] - k * values[k - 1]) * (1.0 / (k + 1.0)))
    return [values[k] * math.sqrt(2.0 * k + 1.0) for k in range(LEVELS)]


def fill_tables(coords_ref, weight, triples, pairs):
    for group, table in enumerate(triples):
        first, second, third = (legendre(coords_ref[3 * group + d]) for d in range(3))
        for a in range(LEVELS):
            for b in range(LEVELS - a):
                head = first[a] * second[b]
                for c in range(LEVELS - a - b):
                    table[a * 49 + b * 7 + c] = head * third[c]
    for group, table in enumerate(pairs):
        first, second = (legendre(coords_ref[6 + 2 * group + d]) for d in range(2))
        if group == 0:
            first = [value * weight for value in first]
        for a in range(LEVELS):
            for b in range(LEVELS - a):
                table[a * 7 + b] = first[a] * second[b]


def table_rows(degree):
    return [
        degree(0) * 49 + degree(1) * 7 + degree(2),
        degree(3) * 49 + degree(4) * 7 + degree(5),
        degree(6) * 7 + degree(7),
        degree(8) * 7 + degree(9),
    ]


def kernel(run_total, points_ref, weights_ref, panel_deg_ref, trail_deg_ref,
           upper_out, coupling_out, updated_out,
           coords, triple_a, triple_b, pair_a, pair_b, columns,
           trail_idx_v, trail_idx, panel_degs, panel_idx_v, panel_idx,
           trail_t, panel_t, out_buf,
           gram_x, gram_land, gram_z, gram_all, cross_x, cross_land, cross_z, cross_all,
           inverse, local_sem, deg_send, deg_recv, send_sem, recv_sem, out_sem):
    s, y = lax.axis_index("sample"), lax.axis_index("basis")
    z, q = s // RING, lax.rem(s, RING)
    others = range(1, RING)
    y_peers = [(s, lax.rem(y + k, RING)) for k in others]
    q_peers = [(z * RING + lax.rem(q + k, RING), y) for k in others]
    z_peers = [(lax.rem(z + k, RING) * RING + q, y) for k in others]

    barrier = pltpu.get_barrier_semaphore()
    for peer in y_peers + z_peers + q_peers:
        pl.semaphore_signal(barrier, inc=1, device_id=peer, device_id_type=MESH)

    def send(src, dst, ssem, rsem, peer):
        pltpu.make_async_remote_copy(
            src_ref=src, dst_ref=dst, send_sem=ssem, recv_sem=rsem, device_id=peer, device_id_type=MESH
        ).start()

    def wait(ref, sem):
        pltpu.make_async_copy(ref, ref, sem).wait()

    for g, row in enumerate(table_rows(lambda d: trail_deg_ref[d:d + 1, :])):
        trail_idx_v[g:g + 1, :] = row
    idx_copy = pltpu.make_async_copy(trail_idx_v, trail_idx, local_sem)
    idx_copy.start()
    for r in range(TILES):
        coords[:, r, :] = points_ref[:, 128 * r:128 * r + 128]
    weight = jnp.sqrt(weights_ref[...] / run_total)
    fill_tables(coords, weight, (triple_a, triple_b), (pair_a, pair_b))
    idx_copy.wait()

    pl.semaphore_wait(barrier, 3 * (RING - 1))
    for peer in y_peers:
        send(panel_deg_ref, panel_degs.at[y], deg_send, deg_recv, peer)
    panel_degs[y] = panel_deg_ref[...]

    def product(i, j, k, m):
        return triple_a[i] * triple_b[j] * (pair_a[k] * pair_b[m])

    def trail_column(j, carry):
        value = product(trail_idx[0, j], trail_idx[1, j], trail_idx[2, j], trail_idx[3, j])
        columns[pl.ds(PANEL + j, TILES, stride=COLS), :] = value
        return carry

    lax.fori_loop(0, TRAIL, trail_column, 0, unroll=8)

    wait(panel_degs.at[pl.ds(0, RING - 1)], deg_recv)
    for g, rows in enumerate(table_rows(lambda d: panel_degs[:, d, :])):
        panel_idx_v[g] = rows
    panel_copy = pltpu.make_async_copy(panel_idx_v, panel_idx, local_sem)
    panel_copy.start()
    panel_copy.wait()

    def panel_column(o, carry):
        for i in range(16):
            value = product(panel_idx[0, o, i], panel_idx[1, o, i], panel_idx[2, o, i], panel_idx[3, o, i])
            columns[pl.ds(o * 16 + i, TILES, stride=COLS), :] = value
        return carry

    lax.fori_loop(0, RING, panel_column, 0)

    def block(start, size, r):
        return jnp.concatenate(
            [columns[pl.ds((2 * r + h) * COLS + start, size), :] for h in range(2)], axis=1
        )

    def phase_one(x, land, i):
        for k in others:
            send(x.at[lax.rem(q + k, RING)], land.at[k - 1], send_sem.at[i], recv_sem.at[i], q_peers[k - 1])

    def phase_two(x, land, all_z, i):
        wait(land, recv_sem.at[i])
        part = x[q]
        for k in range(RING - 1):
            part = part + land[k]
        all_z[z] = part
        for peer in z_peers:
            send(all_z.at[z], all_z.at[z], send_sem.at[i + 1], recv_sem.at[i + 1], peer)

    def phase_three(land, all_z, out, i):
        wait(land, recv_sem.at[i + 1])
        total = all_z[0]
        for k in others:
            total = total + all_z[k]
        out[q] = total
        for peer in q_peers:
            send(out.at[q], out.at[q], send_sem.at[i + 2], recv_sem.at[i + 2], peer)

    gram = jnp.zeros((PANEL, PANEL), jnp.float32)
    for r in range(TILES // 2):
        panel = block(0, PANEL, r)
        gram = gram + dot(panel, panel, NT)
    gram_x[...] = gram.reshape(gram_x.shape)
    phase_one(gram_x, gram_land, 0)
    cross = jnp.zeros((PANEL, TRAIL), jnp.float32)
    for r in range(TILES // 2):
        cross = cross + dot(block(0, PANEL, r), block(PANEL, TRAIL, r), NT)
    cross_x[...] = cross.reshape(cross_x.shape)
    phase_one(cross_x, cross_land, 3)

    def transpose(r, carry):
        rows = pl.ds(pl.multiple_of(r * 128, 128), 128)
        base = pl.multiple_of(r * COLS, 128)
        panel_t[rows, :] = columns[pl.ds(base, PANEL), :].T
        trail_t[rows, :] = columns[pl.ds(base + PANEL, TRAIL), :].T
        return carry

    lax.fori_loop(0, TILES, transpose, 0)
    phase_two(gram_x, gram_land, gram_z, 0)
    phase_two(cross_x, cross_land, cross_z, 3)
    phase_three(gram_land, gram_z, gram_all, 0)
    phase_three(cross_land, cross_z, cross_all, 3)

    wait(gram_land, recv_sem.at[2])
    gram_flat = gram_all.reshape(PANEL, PANEL)
    cholesky(gram_flat, upper_out, inverse)
    wait(cross_land, recv_sem.at[5])
    coupling = dot(inverse[...], cross_all[...].reshape(PANEL, TRAIL), (((1,), (0,)), ((), ())))
    coupling_out[...] = coupling
    weights = dot(inverse[...], coupling, TN)
    scale = math.sqrt(run_total)
    part = 2048 // 4
    for p in range(4):
        rows = pl.ds(p * part, part)
        out_buf[rows, :] = (trail_t[rows, :] - dot(panel_t[rows, :], weights, (((1,), (0,)), ((), ())))) * scale
        pltpu.make_async_copy(out_buf.at[rows, :], updated_out.at[rows, :], out_sem).start()
    wait(panel_degs.at[pl.ds(0, RING - 1)], deg_send)
    for i in range(3):
        wait(gram_land, send_sem.at[i])
        wait(cross_land, send_sem.at[i + 3])
    pltpu.make_async_copy(out_buf, updated_out, out_sem).wait()


def shards(points, run_weights, panel_degrees, trailing_degrees):
    run_total = float(points.shape[1] * lax.axis_size("sample"))
    f32, i32 = jnp.float32, jnp.int32
    vmem = pl.BlockSpec(memory_space=pltpu.VMEM)
    dma = pltpu.SemaphoreType.DMA
    chunk, wide = (16, PANEL), (16, TRAIL)
    return pl.pallas_call(
        functools.partial(kernel, run_total),
        out_shape=[
            jax.ShapeDtypeStruct((PANEL, PANEL), f32),
            jax.ShapeDtypeStruct((PANEL, TRAIL), f32),
            jax.ShapeDtypeStruct((2048, TRAIL), f32),
        ],
        in_specs=[vmem] * 4,
        out_specs=[vmem, vmem, pl.BlockSpec(memory_space=pl.ANY)],
        scratch_shapes=[
            pltpu.VMEM((10, TILES, 128), f32),
            pltpu.VMEM((343, TILES, 128), f32),
            pltpu.VMEM((343, TILES, 128), f32),
            pltpu.VMEM((49, TILES, 128), f32),
            pltpu.VMEM((49, TILES, 128), f32),
            pltpu.VMEM((TILES * COLS, 128), f32),
            pltpu.VMEM((4, TRAIL), i32),
            pltpu.SMEM((4, TRAIL), i32),
            pltpu.VMEM((RING, 10, 16), i32),
            pltpu.VMEM((4, RING, 16), i32),
            pltpu.SMEM((4, RING, 16), i32),
            pltpu.VMEM((2048, TRAIL), f32),
            pltpu.VMEM((2048, PANEL), f32),
            pltpu.VMEM((2048, TRAIL), f32),
            pltpu.VMEM((RING,) + chunk, f32),
            pltpu.VMEM((RING - 1,) + chunk, f32),
            pltpu.VMEM((RING,) + chunk, f32),
            pltpu.VMEM((RING,) + chunk, f32),
            pltpu.VMEM((RING,) + wide, f32),
            pltpu.VMEM((RING - 1,) + wide, f32),
            pltpu.VMEM((RING,) + wide, f32),
            pltpu.VMEM((RING,) + wide, f32),
            pltpu.VMEM((PANEL, PANEL), f32),
            dma,
            dma,
            dma,
            dma((6,)),
            dma((6,)),
            dma,
        ],
        name="panel_step",
        compiler_params=pltpu.CompilerParams(
            collective_id=0, has_side_effects=True, vmem_limit_bytes=40 * 2**20
        ),
    )(points, run_weights.reshape(TILES, 128), panel_degrees, trailing_degrees)


def solution(mesh):
    in_specs = (P(None, "sample"), P("sample"), P(None, "basis"), P(None, "basis"))
    out_specs = (P(), P(None, "basis"), P("sample", "basis"))
    return jax.shard_map(shards, mesh=mesh, in_specs=in_specs, out_specs=out_specs, check_vma=False)
```

```python
import functools
import math

import jax
import jax.numpy as jnp
from jax import lax
from jax.experimental import pallas as pl
from jax.experimental.pallas import tpu as pltpu
from jax.sharding import PartitionSpec as P

DEG = 6
LEVELS = DEG + 1
TILES = 16
PANEL = 128
TRAIL = 256
COLS = PANEL + TRAIL
RING = 8
MESH = pl.DeviceIdType.MESH
HIGHEST = lax.Precision.HIGHEST
NN = (((1,), (0,)), ((), ()))
NT = (((1,), (1,)), ((), ()))
TN = (((0,), (0,)), ((), ()))


def dot(left, right, dims):
    return lax.dot_general(left, right, dims, precision=HIGHEST, preferred_element_type=jnp.float32)


def lane_splat(row, lane):
    return jnp.broadcast_to(row[:, lane:lane + 1], (8, 128))


def sublane_splat(row, sublane):
    return jnp.broadcast_to(row[sublane:sublane + 1, :], (8, 128))


def cholesky(gram_ref, upper_ref, inverse_ref):
    sub = lax.broadcasted_iota(jnp.int32, (8, 128), 0)
    lane = lax.broadcasted_iota(jnp.int32, (8, 128), 1)
    gram = [gram_ref[8 * i:8 * i + 8, :] for i in range(16)]
    ident = [jnp.where(lane == sub + 8 * i, 1.0, 0.0) for i in range(16)]
    for k in range(16):
        splats = [lane_splat(gram[k], 8 * k + j) for j in range(8)]
        diag = [[sublane_splat(splats[j], i) if i >= j else None for j in range(8)] for i in range(8)]
        low = [[None] * 8 for _ in range(8)]
        inv = [None] * 8
        for j in range(8):
            inv[j] = lax.rsqrt(diag[j][j])
            for i in range(j + 1, 8):
                low[i][j] = diag[i][j] * inv[j]
            for i in range(j + 1, 8):
                for m in range(i, 8):
                    diag[m][i] = diag[m][i] - low[m][j] * low[i][j]
        up, lo = [], []
        for j in range(8):
            a, b = sublane_splat(gram[k], j), sublane_splat(ident[k], j)
            for i in range(j):
                a = a - low[j][i] * up[i]
                b = b - low[j][i] * lo[i]
            up.append(a * inv[j])
            lo.append(b * inv[j])
        up_rows, lo_rows = up[0], lo[0]
        for j in range(1, 8):
            up_rows = jnp.where(sub == j, up[j], up_rows)
            lo_rows = jnp.where(sub == j, lo[j], lo_rows)
        upper_ref[8 * k:8 * k + 8, :] = jnp.where(lane >= sub + 8 * k, up_rows, 0.0)
        inverse_ref[8 * k:8 * k + 8, :] = lo_rows
        if k == 15:
            break
        for j in reversed(range(8)):
            for i in range(j + 1, 8):
                up[j] = up[j] - low[i][j] * up[i]
                lo[j] = lo[j] - low[i][j] * lo[i]
            up[j] = up[j] * inv[j]
            lo[j] = lo[j] * inv[j]
        for i in range(k + 1, 16):
            for j in range(8):
                c = lane_splat(gram[i], 8 * k + j)
                if j == 0:
                    a, b = c * up[0], c * lo[0]
                else:
                    a, b = a + c * up[j], b + c * lo[j]
            gram[i] = gram[i] - a
            ident[i] = ident[i] - b


def legendre(coord):
    values = [jnp.ones_like(coord), coord]
    for k in range(1, DEG):
        values.append(((2.0 * k + 1.0) * coord * values[k] - k * values[k - 1]) * (1.0 / (k + 1.0)))
    return [values[k] * math.sqrt(2.0 * k + 1.0) for k in range(LEVELS)]


def fill_tables(coords_ref, weight, triples, pairs):
    for group, table in enumerate(triples):
        first, second, third = (legendre(coords_ref[3 * group + d]) for d in range(3))
        for a in range(LEVELS):
            for b in range(LEVELS - a):
                head = first[a] * second[b]
                for c in range(LEVELS - a - b):
                    table[a * 49 + b * 7 + c] = head * third[c]
    for group, table in enumerate(pairs):
        first, second = (legendre(coords_ref[6 + 2 * group + d]) for d in range(2))
        if group == 0:
            first = [value * weight for value in first]
        for a in range(LEVELS):
            for b in range(LEVELS - a):
                table[a * 7 + b] = first[a] * second[b]


def table_rows(degree):
    return [
        degree(0) * 49 + degree(1) * 7 + degree(2),
        degree(3) * 49 + degree(4) * 7 + degree(5),
        degree(6) * 7 + degree(7),
        degree(8) * 7 + degree(9),
    ]


def split(value):
    high = value.astype(jnp.bfloat16)
    return high, (value - high.astype(jnp.float32)).astype(jnp.bfloat16)


def fast_dot(left, right, dims):
    return lax.dot_general(left, right, dims, preferred_element_type=jnp.float32)


def kernel(run_total, points_ref, weights_ref, panel_deg_ref, trail_deg_ref,
           upper_out, coupling_out, weights_out, trail_t, panel_t,
           points_v, weights_v, panel_deg_v, trail_deg_v,
           coords, triple_a, triple_b, pair_a, pair_b, columns,
           trail_idx_v, trail_idx, panel_degs, panel_idx_v, panel_idx,
           gram_x, gram_land, gram_z, gram_all, cross_x, cross_land, cross_z, cross_all,
           inverse, in_sem, local_sem, deg_send, deg_recv, send_sem, recv_sem):
    s, y = lax.axis_index("sample"), lax.axis_index("basis")
    z, q = s // RING, lax.rem(s, RING)
    others = range(1, RING)
    y_peers = [(s, lax.rem(y + k, RING)) for k in others]
    q_peers = [(z * RING + lax.rem(q + k, RING), y) for k in others]
    z_peers = [(lax.rem(z + k, RING) * RING + q, y) for k in others]

    barrier = pltpu.get_barrier_semaphore()
    for peer in y_peers + z_peers + q_peers:
        pl.semaphore_signal(barrier, inc=1, device_id=peer, device_id_type=MESH)
    loads = [
        pltpu.make_async_copy(src, dst, in_sem.at[i])
        for i, (src, dst) in enumerate([
            (panel_deg_ref, panel_deg_v), (trail_deg_ref, trail_deg_v), (points_ref, points_v), (weights_ref, weights_v)
        ])
    ]
    for load in loads:
        load.start()

    def send(src, dst, ssem, rsem, peer):
        pltpu.make_async_remote_copy(
            src_ref=src, dst_ref=dst, send_sem=ssem, recv_sem=rsem, device_id=peer, device_id_type=MESH
        ).start()

    def wait(ref, sem):
        pltpu.make_async_copy(ref, ref, sem).wait()

    loads[0].wait()
    pl.semaphore_wait(barrier, 3 * (RING - 1))
    for peer in y_peers:
        send(panel_deg_v, panel_degs.at[y], deg_send, deg_recv, peer)
    panel_degs[y] = panel_deg_v[...]

    loads[1].wait()
    for g, row in enumerate(table_rows(lambda d: trail_deg_v[d:d + 1, :])):
        trail_idx_v[g:g + 1, :] = row
    idx_copy = pltpu.make_async_copy(trail_idx_v, trail_idx, local_sem)
    idx_copy.start()
    loads[2].wait()
    loads[3].wait()
    for r in range(TILES):
        coords[:, r, :] = points_v[:, 128 * r:128 * r + 128]
    weight = jnp.sqrt(weights_v[...] / run_total)
    fill_tables(coords, weight, (triple_a, triple_b), (pair_a, pair_b))
    idx_copy.wait()

    def product(i, j, k, m):
        return triple_a[i] * triple_b[j] * (pair_a[k] * pair_b[m])

    def trail_column(j, carry):
        value = product(trail_idx[0, j], trail_idx[1, j], trail_idx[2, j], trail_idx[3, j])
        columns[pl.ds(PANEL + j, TILES, stride=COLS), :] = value
        return carry

    lax.fori_loop(0, TRAIL, trail_column, 0, unroll=8)
    scale = math.sqrt(run_total)

    def transpose_trail(r, carry):
        rows = pl.ds(pl.multiple_of(r * 128, 128), 128)
        base = pl.multiple_of(r * COLS, 128)
        trail_t[rows, :] = columns[pl.ds(base + PANEL, TRAIL), :].T * scale
        return carry

    lax.fori_loop(0, TILES, transpose_trail, 0)

    wait(panel_degs.at[pl.ds(0, RING - 1)], deg_recv)
    for g, rows in enumerate(table_rows(lambda d: panel_degs[:, d, :])):
        panel_idx_v[g] = rows
    panel_copy = pltpu.make_async_copy(panel_idx_v, panel_idx, local_sem)
    panel_copy.start()
    panel_copy.wait()

    def panel_column(o, carry):
        for i in range(16):
            value = product(panel_idx[0, o, i], panel_idx[1, o, i], panel_idx[2, o, i], panel_idx[3, o, i])
            columns[pl.ds(o * 16 + i, TILES, stride=COLS), :] = value
        return carry

    lax.fori_loop(0, RING, panel_column, 0)

    def block(start, size, r):
        high, low = split(jnp.concatenate(
            [columns[pl.ds((2 * r + h) * COLS + start, size), :] for h in range(2)], axis=1
        ))
        return jnp.concatenate([high, low], axis=0)

    def quadrants(total):
        rows, cols = total.shape[0] // 2, total.shape[1] // 2
        return (total[rows:, cols:] + (total[:rows, cols:] + total[rows:, :cols])) + total[:rows, :cols]

    def phase_one(x, land, i):
        for k in others:
            send(x.at[lax.rem(q + k, RING)], land.at[k - 1], send_sem.at[i], recv_sem.at[i], q_peers[k - 1])

    def phase_two(x, land, all_z, i):
        wait(land, recv_sem.at[i])
        part = x[q]
        for k in range(RING - 1):
            part = part + land[k]
        all_z[z] = part
        for peer in z_peers:
            send(all_z.at[z], all_z.at[z], send_sem.at[i + 1], recv_sem.at[i + 1], peer)

    def phase_three(land, all_z, out, i):
        wait(land, recv_sem.at[i + 1])
        total = all_z[0]
        for k in others:
            total = total + all_z[k]
        out[q] = total
        for peer in q_peers:
            send(out.at[q], out.at[q], send_sem.at[i + 2], recv_sem.at[i + 2], peer)

    panels = [block(0, PANEL, r) for r in range(TILES // 2)]
    gram = fast_dot(panels[0], panels[0], NT)
    for r in range(1, TILES // 2):
        gram = gram + fast_dot(panels[r], panels[r], NT)
    gram_x[...] = quadrants(gram).reshape(gram_x.shape)
    phase_one(gram_x, gram_land, 0)
    cross = jnp.zeros((2 * PANEL, 2 * TRAIL), jnp.float32)
    for r in range(TILES // 2):
        cross = cross + fast_dot(panels[r], block(PANEL, TRAIL, r), NT)
    cross_x[...] = quadrants(cross).reshape(cross_x.shape)
    phase_one(cross_x, cross_land, 3)

    def transpose_panel(r, carry):
        rows = pl.ds(pl.multiple_of(r * 128, 128), 128)
        base = pl.multiple_of(r * COLS, 128)
        high, low = split(columns[pl.ds(base, PANEL), :].T)
        panel_t[rows, :] = jnp.concatenate([high, low], axis=1)
        return carry

    lax.fori_loop(0, TILES, transpose_panel, 0)
    phase_two(gram_x, gram_land, gram_z, 0)
    phase_two(cross_x, cross_land, cross_z, 3)
    phase_three(gram_land, gram_z, gram_all, 0)
    phase_three(cross_land, cross_z, cross_all, 3)

    wait(gram_land, recv_sem.at[2])
    cholesky(gram_all.reshape(PANEL, PANEL), upper_out, inverse)
    wait(cross_land, recv_sem.at[5])
    coupling = dot(inverse[...], cross_all[...].reshape(PANEL, TRAIL), NN)
    coupling_out[...] = coupling
    weights_out[...] = dot(inverse[...], coupling, TN) * -scale
    wait(panel_degs.at[pl.ds(0, RING - 1)], deg_send)
    for i in range(3):
        wait(gram_land, send_sem.at[i])
        wait(cross_land, send_sem.at[i + 3])


def update_kernel(upper_ref, coupling_ref, weights_ref, trail_t, panel_t, upper_out, coupling_out, updated_out, buf, sem):
    small = [
        pltpu.make_async_copy(upper_ref, upper_out, sem.at[0]),
        pltpu.make_async_copy(coupling_ref, coupling_out, sem.at[1]),
    ]
    for copy in small:
        copy.start()
    high, low = split(weights_ref[...])
    both = jnp.concatenate([high, high], axis=0)
    part = 2048 // 4
    large = []
    for p in range(4):
        rows = pl.ds(p * part, part)
        panel = panel_t[rows, :]
        buf[rows, :] = trail_t[rows, :] + (fast_dot(panel[:, :PANEL], low, NN) + fast_dot(panel, both, NN))
        large.append(pltpu.make_async_copy(buf.at[rows, :], updated_out.at[rows, :], sem.at[2 + p]))
        large[-1].start()
    for copy in small + large:
        copy.wait()


def shards(points, run_weights, panel_degrees, trailing_degrees):
    run_total = float(points.shape[1] * lax.axis_size("sample"))
    f32, i32 = jnp.float32, jnp.int32
    vmem, hbm = pl.BlockSpec(memory_space=pltpu.VMEM), pl.BlockSpec(memory_space=pltpu.HBM)
    dma = pltpu.SemaphoreType.DMA
    chunk, wide = (16, PANEL), (16, TRAIL)
    upper = jax.ShapeDtypeStruct((PANEL, PANEL), f32)
    coupling = jax.ShapeDtypeStruct((PANEL, TRAIL), f32)
    updated = jax.ShapeDtypeStruct((2048, TRAIL), f32)
    parts = pl.pallas_call(
        functools.partial(kernel, run_total),
        out_shape=[upper, coupling, coupling, updated, jax.ShapeDtypeStruct((2048, 2 * PANEL), jnp.bfloat16)],
        in_specs=[hbm] * 4,
        out_specs=[vmem] * 5,
        scratch_shapes=[
            pltpu.VMEM((10, 2048), f32),
            pltpu.VMEM((TILES, 128), f32),
            pltpu.VMEM((10, 16), i32),
            pltpu.VMEM((10, TRAIL), i32),
            pltpu.VMEM((10, TILES, 128), f32),
            pltpu.VMEM((343, TILES, 128), f32),
            pltpu.VMEM((343, TILES, 128), f32),
            pltpu.VMEM((49, TILES, 128), f32),
            pltpu.VMEM((49, TILES, 128), f32),
            pltpu.VMEM((TILES * COLS, 128), f32),
            pltpu.VMEM((4, TRAIL), i32),
            pltpu.SMEM((4, TRAIL), i32),
            pltpu.VMEM((RING, 10, 16), i32),
            pltpu.VMEM((4, RING, 16), i32),
            pltpu.SMEM((4, RING, 16), i32),
            pltpu.VMEM((RING,) + chunk, f32),
            pltpu.VMEM((RING - 1,) + chunk, f32),
            pltpu.VMEM((RING,) + chunk, f32),
            pltpu.VMEM((RING,) + chunk, f32),
            pltpu.VMEM((RING,) + wide, f32),
            pltpu.VMEM((RING - 1,) + wide, f32),
            pltpu.VMEM((RING,) + wide, f32),
            pltpu.VMEM((RING,) + wide, f32),
            pltpu.VMEM((PANEL, PANEL), f32),
            dma((4,)),
            dma,
            dma,
            dma,
            dma((6,)),
            dma((6,)),
        ],
        name="panel_step",
        compiler_params=pltpu.CompilerParams(
            collective_id=0, has_side_effects=True, vmem_limit_bytes=32 * 2**20
        ),
    )(*(pltpu.with_memory_space_constraint(a, pltpu.HBM) for a in (
        points, run_weights.reshape(TILES, 128), panel_degrees, trailing_degrees
    )))
    return pl.pallas_call(
        update_kernel,
        out_shape=[upper, coupling, updated],
        in_specs=[vmem] * 5,
        out_specs=[hbm] * 3,
        scratch_shapes=[pltpu.VMEM((2048, TRAIL), f32), dma((6,))],
        name="update_step",
        compiler_params=pltpu.CompilerParams(vmem_limit_bytes=16 * 2**20),
    )(*parts)


def solution(mesh):
    in_specs = (P(None, "sample"), P("sample"), P(None, "basis"), P(None, "basis"))
    out_specs = (P(), P(None, "basis"), P("sample", "basis"))
    return jax.shard_map(shards, mesh=mesh, in_specs=in_specs, out_specs=out_specs, check_vma=False)
```

```python
import functools
import math

import jax
import jax.numpy as jnp
from jax import lax
from jax.experimental import pallas as pl
from jax.experimental.pallas import tpu as pltpu
from jax.sharding import PartitionSpec as P

DEG = 6
LEVELS = DEG + 1
TILES = 16
PANEL = 128
TRAIL = 256
COLS = PANEL + TRAIL
PITCH = COLS + 8
FAR_FIRST = (4, 3, 5, 2, 6, 1, 7)
RING = 8
MESH = pl.DeviceIdType.MESH
NN = (((1,), (0,)), ((), ()))
NT = (((1,), (1,)), ((), ()))
TN = (((0,), (0,)), ((), ()))


def lane_splat(row, lane):
    return jnp.broadcast_to(row[:, lane:lane + 1], (8, 128))


def cholesky(gram_ref, upper_ref, inverse_ref, rows_ref):
    sub = lax.broadcasted_iota(jnp.int32, (8, 128), 0)
    lane = lax.broadcasted_iota(jnp.int32, (8, 128), 1)
    rows = [gram_ref[8 * i:8 * i + 8, :] for i in range(16)]

    def all_sublanes(row):
        return jnp.broadcast_to(rows_ref[row:row + 1, :], (8, 128))

    for k in range(16):
        first, last = 8 * k, k == 15
        mid = (lane >= first) & (lane < first + 8)
        for j in range(8):
            rows_ref[8 * j:8 * j + 8, :] = lane_splat(rows[k], first + j)
        rows_ref[64:72, :] = rows[k]
        diag = [[all_sublanes(8 * j + i) if i >= j else None for j in range(8)] for i in range(8)]
        up = [all_sublanes(64 + j) for j in range(8)]
        lo = [jnp.where(mid, jnp.where(lane == first + j, 1.0, 0.0), up[j]) for j in range(8)]
        following = None if last else [lane_splat(rows[k + 1], first + j) for j in range(8)]
        low = [[None] * 8 for _ in range(8)]
        inv = [None] * 8
        change = None
        for j in range(8):
            inv[j] = lax.rsqrt(diag[j][j])
            up[j] = up[j] * inv[j]
            lo[j] = lo[j] * inv[j]
            for i in range(j + 1, 8):
                low[i][j] = diag[i][j] * inv[j]
            if not last:
                following[j] = following[j] * inv[j]
                term = following[j] * lo[j]
                change = term if change is None else change + term
            for i in range(j + 1, 8):
                for m in range(i, 8):
                    diag[m][i] = diag[m][i] - low[m][j] * low[i][j]
                up[i] = up[i] - low[i][j] * up[j]
                lo[i] = lo[i] - low[i][j] * lo[j]
                if not last:
                    following[i] = following[i] - low[i][j] * following[j]
        up_rows, lo_rows = up[0], lo[0]
        for j in range(1, 8):
            up_rows = jnp.where(sub == j, up[j], up_rows)
            lo_rows = jnp.where(sub == j, lo[j], lo_rows)
        upper_ref[first:first + 8, :] = jnp.where(lane >= sub + first, up_rows, 0.0)
        inverse_ref[first:first + 8, :] = jnp.where(lane < first + 8, lo_rows, 0.0)
        if last:
            break
        rows[k + 1] = jnp.where(mid, 0.0, rows[k + 1]) - change
        if k == 14:
            continue
        for j in reversed(range(8)):
            lo[j] = lo[j] * inv[j]
            for i in range(j):
                lo[i] = lo[i] - low[j][i] * lo[j]
        for i in range(k + 2, 16):
            kept = jnp.where(mid, 0.0, rows[i])
            for j in range(8):
                kept = kept - lane_splat(rows[i], first + j) * lo[j]
            rows[i] = kept


def legendre(coord):
    values = [jnp.ones_like(coord), coord]
    for k in range(1, DEG):
        values.append(((2.0 * k + 1.0) * coord * values[k] - k * values[k - 1]) * (1.0 / (k + 1.0)))
    return [values[k] * math.sqrt(2.0 * k + 1.0) for k in range(LEVELS)]


def fill_tables(coords_ref, weight, triples, pairs):
    for group, table in enumerate(triples):
        first, second, third = (legendre(coords_ref[3 * group + d]) for d in range(3))
        for a in range(LEVELS):
            for b in range(LEVELS - a):
                head = first[a] * second[b]
                for c in range(LEVELS - a - b):
                    table[a * 49 + b * 7 + c] = head * third[c]
    for group, table in enumerate(pairs):
        first, second = (legendre(coords_ref[6 + 2 * group + d]) for d in range(2))
        if group == 0:
            first = [value * weight for value in first]
        for a in range(LEVELS):
            for b in range(LEVELS - a):
                table[a * 7 + b] = first[a] * second[b]


def table_rows(degree):
    return [
        degree(0) * 49 + degree(1) * 7 + degree(2),
        degree(3) * 49 + degree(4) * 7 + degree(5),
        degree(6) * 7 + degree(7),
        degree(8) * 7 + degree(9),
    ]


def split(value):
    high = value.astype(jnp.bfloat16)
    return high, (value - high.astype(jnp.float32)).astype(jnp.bfloat16)


def fast_dot(left, right, dims):
    return lax.dot_general(left, right, dims, preferred_element_type=jnp.float32)


def kernel(run_total, points_ref, weights_ref, panel_deg_ref, trail_deg_ref,
           upper_out, coupling_out, weights_out, trail_t, panel_t,
           points_v, weights_v, trail_deg_v,
           coords, triple_a, triple_b, pair_a, pair_b, columns,
           trail_idx_v, trail_idx, panel_degs,
           gram_x, gram_land, gram_z, gram_all, cross_x, cross_land, cross_z, cross_all,
           inverse, rows_v, in_sem, local_sem, deg_send, deg_recv, send_sem, recv_sem):
    s, y = lax.axis_index("sample"), lax.axis_index("basis")
    z, q = s // RING, lax.rem(s, RING)
    others = range(1, RING)
    y_peers = [(s, lax.rem(y + k, RING)) for k in others]
    q_peers = [(z * RING + lax.rem(q + k, RING), y) for k in others]
    z_peers = [(lax.rem(z + k, RING) * RING + q, y) for k in others]

    barrier = pltpu.get_barrier_semaphore()
    for k in FAR_FIRST:
        for peers in (y_peers, z_peers, q_peers):
            pl.semaphore_signal(barrier, inc=1, device_id=peers[k - 1], device_id_type=MESH)
    loads = [
        pltpu.make_async_copy(src, dst, in_sem.at[i])
        for i, (src, dst) in enumerate([
            (panel_deg_ref, panel_degs.at[y]), (trail_deg_ref, trail_deg_v), (points_ref, points_v), (weights_ref, weights_v)
        ])
    ]
    for load in loads:
        load.start()

    def send(src, dst, ssem, rsem, peer):
        pltpu.make_async_remote_copy(
            src_ref=src, dst_ref=dst, send_sem=ssem, recv_sem=rsem, device_id=peer, device_id_type=MESH
        ).start()

    def wait(ref, sem):
        pltpu.make_async_copy(ref, ref, sem).wait()

    loads[0].wait()
    pl.semaphore_wait(barrier, 3 * (RING - 1))
    for k in FAR_FIRST:
        send(panel_degs.at[y], panel_degs.at[y], deg_send.at[k - 1], deg_recv.at[k - 1], y_peers[k - 1])

    loads[1].wait()
    for g, row in enumerate(table_rows(lambda d: trail_deg_v[d:d + 1, :])):
        trail_idx_v[g:g + 1, :] = row
    idx_copy = pltpu.make_async_copy(trail_idx_v, trail_idx, local_sem)
    idx_copy.start()
    loads[2].wait()
    loads[3].wait()
    for r in range(TILES):
        coords[:, r, :] = points_v[:, 128 * r:128 * r + 128]
    weight = jnp.sqrt(weights_v[...] / run_total)
    fill_tables(coords, weight, (triple_a, triple_b), (pair_a, pair_b))
    idx_copy.wait()

    def product(i, j, k, m):
        return triple_a[i] * triple_b[j] * (pair_a[k] * pair_b[m])

    def trail_column(j, carry):
        value = product(trail_idx[0, j], trail_idx[1, j], trail_idx[2, j], trail_idx[3, j])
        columns[pl.ds(PANEL + j, TILES, stride=PITCH), :] = value
        return carry

    lax.fori_loop(0, TRAIL, trail_column, 0, unroll=8)

    def panel_block(owner):
        def panel_column(i, carry):
            rows = table_rows(lambda d: panel_degs[owner, d, i])
            columns[pl.ds(owner * 16 + i, TILES, stride=PITCH), :] = product(*rows)
            return carry

        lax.fori_loop(0, 16, panel_column, 0, unroll=4)

    panel_block(y)
    for k in (1, 7, 2, 6, 3, 5, 4):
        owner = lax.rem(y + RING - k, RING)
        wait(panel_degs.at[owner], deg_recv.at[k - 1])
        panel_block(owner)

    def block(start, size, r):
        high, low = split(jnp.concatenate(
            [columns[pl.ds((2 * r + h) * PITCH + start, size), :] for h in range(2)], axis=1
        ))
        return jnp.concatenate([high, low], axis=0)

    def quadrants(total):
        rows, cols = total.shape[0] // 2, total.shape[1] // 2
        return (total[rows:, cols:] + (total[:rows, cols:] + total[rows:, :cols])) + total[:rows, :cols]

    def phase_one(x, land, i):
        for k in FAR_FIRST:
            send(x.at[lax.rem(q + k, RING)], land.at[k - 1], send_sem.at[i], recv_sem.at[i], q_peers[k - 1])

    def phase_two(x, land, all_z, i):
        wait(land, recv_sem.at[i])
        part = x[q]
        for k in range(RING - 1):
            part = part + land[k]
        all_z[z] = part
        for k in FAR_FIRST:
            send(all_z.at[z], all_z.at[z], send_sem.at[i + 1], recv_sem.at[i + 1], z_peers[k - 1])

    def phase_three(land, all_z, out, i):
        wait(land, recv_sem.at[i + 1])
        total = all_z[0]
        for k in others:
            total = total + all_z[k]
        out[q] = total
        for k in FAR_FIRST:
            send(out.at[q], out.at[q], send_sem.at[i + 2], recv_sem.at[i + 2], q_peers[k - 1])

    panels = [block(0, PANEL, r) for r in range(TILES // 2)]
    gram = fast_dot(panels[0], panels[0], NT)
    for r in range(1, TILES // 2):
        gram = gram + fast_dot(panels[r], panels[r], NT)
    gram_x[...] = quadrants(gram).reshape(gram_x.shape)
    phase_one(gram_x, gram_land, 0)
    cross = jnp.zeros((2 * PANEL, 2 * TRAIL), jnp.float32)
    for r in range(TILES // 2):
        cross = cross + fast_dot(panels[r], block(PANEL, TRAIL, r), NT)
    cross_x[...] = quadrants(cross).reshape(cross_x.shape)
    phase_one(cross_x, cross_land, 3)

    scale = math.sqrt(run_total)

    def transpose(r, carry):
        rows = pl.ds(pl.multiple_of(r * 128, 128), 128)
        base = pl.multiple_of(r * PITCH, 8)
        high, low = split(columns[pl.ds(base, PANEL), :].T)
        panel_t[rows, :] = jnp.concatenate([high, low], axis=1)
        trail_t[rows, :] = columns[pl.ds(base + PANEL, TRAIL), :].T * scale
        return carry

    phase_two(gram_x, gram_land, gram_z, 0)
    phase_two(cross_x, cross_land, cross_z, 3)
    lax.fori_loop(0, TILES, transpose, 0)
    phase_three(gram_land, gram_z, gram_all, 0)
    phase_three(cross_land, cross_z, cross_all, 3)

    wait(gram_land, recv_sem.at[2])
    cholesky(gram_all.reshape(PANEL, PANEL), upper_out, inverse, rows_v)
    wait(cross_land, recv_sem.at[5])
    inv_high, inv_low = split(inverse[...])
    high, low = split(cross_all[...].reshape(PANEL, TRAIL))
    coupling = fast_dot(inv_high, high, NN) + (fast_dot(inv_high, low, NN) + fast_dot(inv_low, high, NN))
    coupling_out[...] = coupling
    high, low = split(coupling)
    weights = fast_dot(inv_high, high, TN) + (fast_dot(inv_high, low, TN) + fast_dot(inv_low, high, TN))
    weights_out[...] = weights * -scale
    for k in others:
        wait(panel_degs.at[y], deg_send.at[k - 1])
    for i in range(3):
        wait(gram_land, send_sem.at[i])
        wait(cross_land, send_sem.at[i + 3])


def update_kernel(upper_ref, coupling_ref, weights_ref, trail_t, panel_t, upper_out, coupling_out, updated_out, buf, sem):
    small = [
        pltpu.make_async_copy(upper_ref, upper_out, sem.at[0]),
        pltpu.make_async_copy(coupling_ref, coupling_out, sem.at[1]),
    ]
    for copy in small:
        copy.start()
    high, low = split(weights_ref[...])
    both = jnp.concatenate([high, high], axis=0)
    part = 2048 // 8
    large = []
    for p in range(8):
        rows = pl.ds(p * part, part)
        panel = panel_t[rows, :]
        buf[rows, :] = trail_t[rows, :] + (fast_dot(panel[:, :PANEL], low, NN) + fast_dot(panel, both, NN))
        large.append(pltpu.make_async_copy(buf.at[rows, :], updated_out.at[rows, :], sem.at[2 + p]))
        large[-1].start()
    for copy in small + large:
        copy.wait()


def shards(points, run_weights, panel_degrees, trailing_degrees):
    run_total = float(points.shape[1] * lax.axis_size("sample"))
    f32, i32 = jnp.float32, jnp.int32
    vmem, hbm = pl.BlockSpec(memory_space=pltpu.VMEM), pl.BlockSpec(memory_space=pltpu.HBM)
    dma = pltpu.SemaphoreType.DMA
    chunk, wide = (16, PANEL), (16, TRAIL)
    upper = jax.ShapeDtypeStruct((PANEL, PANEL), f32)
    coupling = jax.ShapeDtypeStruct((PANEL, TRAIL), f32)
    updated = jax.ShapeDtypeStruct((2048, TRAIL), f32)
    parts = pl.pallas_call(
        functools.partial(kernel, run_total),
        out_shape=[upper, coupling, coupling, updated, jax.ShapeDtypeStruct((2048, 2 * PANEL), jnp.bfloat16)],
        in_specs=[hbm] * 4,
        out_specs=[vmem] * 5,
        scratch_shapes=[
            pltpu.VMEM((10, 2048), f32),
            pltpu.VMEM((TILES, 128), f32),
            pltpu.VMEM((10, TRAIL), i32),
            pltpu.VMEM((10, TILES, 128), f32),
            pltpu.VMEM((343, TILES, 128), f32),
            pltpu.VMEM((343, TILES, 128), f32),
            pltpu.VMEM((49, TILES, 128), f32),
            pltpu.VMEM((49, TILES, 128), f32),
            pltpu.VMEM((TILES * PITCH, 128), f32),
            pltpu.VMEM((4, TRAIL), i32),
            pltpu.SMEM((4, TRAIL), i32),
            pltpu.SMEM((RING, 10, 16), i32),
            pltpu.VMEM((RING,) + chunk, f32),
            pltpu.VMEM((RING - 1,) + chunk, f32),
            pltpu.VMEM((RING,) + chunk, f32),
            pltpu.VMEM((RING,) + chunk, f32),
            pltpu.VMEM((RING,) + wide, f32),
            pltpu.VMEM((RING - 1,) + wide, f32),
            pltpu.VMEM((RING,) + wide, f32),
            pltpu.VMEM((RING,) + wide, f32),
            pltpu.VMEM((PANEL, PANEL), f32),
            pltpu.VMEM((72, 128), f32),
            dma((4,)),
            dma,
            dma((RING - 1,)),
            dma((RING - 1,)),
            dma((6,)),
            dma((6,)),
        ],
        name="panel_step",
        compiler_params=pltpu.CompilerParams(
            collective_id=0, has_side_effects=True, vmem_limit_bytes=32 * 2**20
        ),
    )(*(pltpu.with_memory_space_constraint(a, pltpu.HBM) for a in (
        points, run_weights.reshape(TILES, 128), panel_degrees, trailing_degrees
    )))
    return pl.pallas_call(
        update_kernel,
        out_shape=[upper, coupling, updated],
        in_specs=[vmem] * 5,
        out_specs=[hbm] * 3,
        scratch_shapes=[pltpu.VMEM((2048, TRAIL), f32), dma((10,))],
        name="update_step",
        compiler_params=pltpu.CompilerParams(vmem_limit_bytes=16 * 2**20),
    )(*parts)


def solution(mesh):
    in_specs = (P(None, "sample"), P("sample"), P(None, "basis"), P(None, "basis"))
    out_specs = (P(), P(None, "basis"), P("sample", "basis"))
    return jax.shard_map(shards, mesh=mesh, in_specs=in_specs, out_specs=out_specs, check_vma=False)
```

```python
import functools
import math

import jax
import jax.numpy as jnp
from jax import lax
from jax.experimental import pallas as pl
from jax.experimental.pallas import tpu as pltpu
from jax.sharding import PartitionSpec as P

DEG = 6
LEVELS = DEG + 1
TILES = 16
PANEL = 128
TRAIL = 256
COLS = PANEL + TRAIL
PITCH = COLS + 8
FAR_FIRST = (4, 3, 5, 2, 6, 1, 7)
RING = 8
MESH = pl.DeviceIdType.MESH
NN = (((1,), (0,)), ((), ()))
NT = (((1,), (1,)), ((), ()))
TN = (((0,), (0,)), ((), ()))


def lane_splat(row, lane):
    return jnp.broadcast_to(row[:, lane:lane + 1], (8, 128))


def cholesky(gram_ref, upper_ref, inverse_ref, rows_ref):
    sub = lax.broadcasted_iota(jnp.int32, (8, 128), 0)
    lane = lax.broadcasted_iota(jnp.int32, (8, 128), 1)
    rows = [gram_ref[8 * i:8 * i + 8, :] for i in range(16)]

    def all_sublanes(row):
        return jnp.broadcast_to(rows_ref[row:row + 1, :], (8, 128))

    for k in range(16):
        first, last = 8 * k, k == 15
        mid = (lane >= first) & (lane < first + 8)
        for j in range(8):
            rows_ref[8 * j:8 * j + 8, :] = lane_splat(rows[k], first + j)
        rows_ref[64:72, :] = rows[k]
        diag = [[all_sublanes(8 * j + i) if i >= j else None for j in range(8)] for i in range(8)]
        up = [all_sublanes(64 + j) for j in range(8)]
        lo = [jnp.where(mid, jnp.where(lane == first + j, 1.0, 0.0), up[j]) for j in range(8)]
        following = None if last else [lane_splat(rows[k + 1], first + j) for j in range(8)]
        low = [[None] * 8 for _ in range(8)]
        inv = [None] * 8
        change = None
        for j in range(8):
            inv[j] = lax.rsqrt(diag[j][j])
            up[j] = up[j] * inv[j]
            lo[j] = lo[j] * inv[j]
            for i in range(j + 1, 8):
                low[i][j] = diag[i][j] * inv[j]
            if not last:
                following[j] = following[j] * inv[j]
                term = following[j] * lo[j]
                change = term if change is None else change + term
            for i in range(j + 1, 8):
                for m in range(i, 8):
                    diag[m][i] = diag[m][i] - low[m][j] * low[i][j]
                up[i] = up[i] - low[i][j] * up[j]
                lo[i] = lo[i] - low[i][j] * lo[j]
                if not last:
                    following[i] = following[i] - low[i][j] * following[j]
        up_rows, lo_rows = up[0], lo[0]
        for j in range(1, 8):
            up_rows = jnp.where(sub == j, up[j], up_rows)
            lo_rows = jnp.where(sub == j, lo[j], lo_rows)
        upper_ref[first:first + 8, :] = jnp.where(lane >= sub + first, up_rows, 0.0)
        inverse_ref[first:first + 8, :] = jnp.where(lane < first + 8, lo_rows, 0.0)
        if last:
            break
        rows[k + 1] = jnp.where(mid, 0.0, rows[k + 1]) - change
        if k == 14:
            continue
        for j in reversed(range(8)):
            lo[j] = lo[j] * inv[j]
            for i in range(j):
                lo[i] = lo[i] - low[j][i] * lo[j]
        for i in range(k + 2, 16):
            kept = jnp.where(mid, 0.0, rows[i])
            for j in range(8):
                kept = kept - lane_splat(rows[i], first + j) * lo[j]
            rows[i] = kept


def legendre(coord):
    values = [jnp.ones_like(coord), coord]
    for k in range(1, DEG):
        values.append(((2.0 * k + 1.0) * coord * values[k] - k * values[k - 1]) * (1.0 / (k + 1.0)))
    return [values[k] * math.sqrt(2.0 * k + 1.0) for k in range(LEVELS)]


def fill_tables(coords_ref, weight, triples, pairs):
    for group, table in enumerate(triples):
        first, second, third = (legendre(coords_ref[3 * group + d]) for d in range(3))
        for a in range(LEVELS):
            for b in range(LEVELS - a):
                head = first[a] * second[b]
                for c in range(LEVELS - a - b):
                    table[a * 49 + b * 7 + c] = head * third[c]
    for group, table in enumerate(pairs):
        first, second = (legendre(coords_ref[6 + 2 * group + d]) for d in range(2))
        if group == 0:
            first = [value * weight for value in first]
        for a in range(LEVELS):
            for b in range(LEVELS - a):
                table[a * 7 + b] = first[a] * second[b]


def table_rows(degree):
    return [
        degree(0) * 49 + degree(1) * 7 + degree(2),
        degree(3) * 49 + degree(4) * 7 + degree(5),
        degree(6) * 7 + degree(7),
        degree(8) * 7 + degree(9),
    ]


def split(value):
    high = value.astype(jnp.bfloat16)
    return high, (value - high.astype(jnp.float32)).astype(jnp.bfloat16)


def fast_dot(left, right, dims):
    return lax.dot_general(left, right, dims, preferred_element_type=jnp.float32)


def kernel(run_total, points_ref, weights_ref, panel_deg_ref, trail_deg_ref,
           upper_out, coupling_out, weights_out, trail_t, panel_t,
           points_v, weights_v, trail_deg_v,
           coords, triple_a, triple_b, pair_a, pair_b, columns,
           trail_idx_v, trail_idx, panel_degs,
           gram_x, gram_land, gram_z, gram_all, cross_x, cross_land, cross_z, cross_all,
           inverse, rows_v, in_sem, local_sem, deg_send, deg_recv, send_sem, recv_sem):
    s, y = lax.axis_index("sample"), lax.axis_index("basis")
    z, q = s // RING, lax.rem(s, RING)
    others = range(1, RING)
    y_peers = [(s, lax.rem(y + k, RING)) for k in others]
    q_peers = [(z * RING + lax.rem(q + k, RING), y) for k in others]
    z_peers = [(lax.rem(z + k, RING) * RING + q, y) for k in others]

    barrier = pltpu.get_barrier_semaphore()
    for k in FAR_FIRST:
        for peers in (y_peers, z_peers, q_peers):
            pl.semaphore_signal(barrier, inc=1, device_id=peers[k - 1], device_id_type=MESH)
    loads = [
        pltpu.make_async_copy(src, dst, in_sem.at[i])
        for i, (src, dst) in enumerate([
            (panel_deg_ref, panel_degs.at[y]), (trail_deg_ref, trail_deg_v), (points_ref, points_v), (weights_ref, weights_v)
        ])
    ]
    for load in loads:
        load.start()

    def send(src, dst, ssem, rsem, peer):
        pltpu.make_async_remote_copy(
            src_ref=src, dst_ref=dst, send_sem=ssem, recv_sem=rsem, device_id=peer, device_id_type=MESH
        ).start()

    def wait(ref, sem):
        pltpu.make_async_copy(ref, ref, sem).wait()

    away = jnp.minimum(y, RING - y)

    def exchange_degrees(now):
        @pl.when(now)
        def _():
            loads[0].wait()
            pl.semaphore_wait(barrier, 3 * (RING - 1))
            for k in FAR_FIRST:
                send(panel_degs.at[y], panel_degs.at[y], deg_send.at[k - 1], deg_recv.at[k - 1], y_peers[k - 1])

    exchange_degrees(away >= 3)

    loads[1].wait()
    for g, row in enumerate(table_rows(lambda d: trail_deg_v[d:d + 1, :])):
        trail_idx_v[g:g + 1, :] = row
    idx_copy = pltpu.make_async_copy(trail_idx_v, trail_idx, local_sem)
    idx_copy.start()
    loads[2].wait()
    loads[3].wait()
    for r in range(TILES):
        coords[:, r, :] = points_v[:, 128 * r:128 * r + 128]
    weight = jnp.sqrt(weights_v[...] / run_total)
    fill_tables(coords, weight, (triple_a, triple_b), (pair_a, pair_b))
    exchange_degrees(jnp.logical_and(away > 0, away < 3))
    idx_copy.wait()

    def product(i, j, k, m):
        return triple_a[i] * triple_b[j] * (pair_a[k] * pair_b[m])

    def trail_column(j, carry):
        value = product(trail_idx[0, j], trail_idx[1, j], trail_idx[2, j], trail_idx[3, j])
        columns[pl.ds(PANEL + j, TILES, stride=PITCH), :] = value
        return carry

    lax.fori_loop(0, TRAIL, trail_column, 0, unroll=8)
    exchange_degrees(away == 0)

    def panel_block(owner):
        def panel_column(i, carry):
            rows = table_rows(lambda d: panel_degs[owner, d, i])
            columns[pl.ds(owner * 16 + i, TILES, stride=PITCH), :] = product(*rows)
            return carry

        lax.fori_loop(0, 16, panel_column, 0, unroll=4)

    panel_block(y)
    for k in (1, 7, 2, 6, 3, 5, 4):
        owner = lax.rem(y + RING - k, RING)
        wait(panel_degs.at[owner], deg_recv.at[k - 1])
        panel_block(owner)

    def block(start, size, r):
        high, low = split(jnp.concatenate(
            [columns[pl.ds((2 * r + h) * PITCH + start, size), :] for h in range(2)], axis=1
        ))
        return jnp.concatenate([high, low], axis=0)

    def quadrants(total):
        rows, cols = total.shape[0] // 2, total.shape[1] // 2
        return (total[rows:, cols:] + (total[:rows, cols:] + total[rows:, :cols])) + total[:rows, :cols]

    def phase_one(x, land, i):
        for k in FAR_FIRST:
            send(x.at[lax.rem(q + k, RING)], land.at[k - 1], send_sem.at[i], recv_sem.at[i], q_peers[k - 1])

    def phase_two(x, land, all_z, i):
        wait(land, recv_sem.at[i])
        part = x[q]
        for k in range(RING - 1):
            part = part + land[k]
        all_z[z] = part
        for k in FAR_FIRST:
            send(all_z.at[z], all_z.at[z], send_sem.at[i + 1], recv_sem.at[i + 1], z_peers[k - 1])

    def phase_three(land, all_z, out, i):
        wait(land, recv_sem.at[i + 1])
        total = all_z[0]
        for k in others:
            total = total + all_z[k]
        out[q] = total
        for k in FAR_FIRST:
            send(out.at[q], out.at[q], send_sem.at[i + 2], recv_sem.at[i + 2], q_peers[k - 1])

    panels = [block(0, PANEL, r) for r in range(TILES // 2)]
    gram = fast_dot(panels[0], panels[0], NT)
    for r in range(1, TILES // 2):
        gram = gram + fast_dot(panels[r], panels[r], NT)
    gram_x[...] = quadrants(gram).reshape(gram_x.shape)
    phase_one(gram_x, gram_land, 0)
    cross = jnp.zeros((2 * PANEL, 2 * TRAIL), jnp.float32)
    for r in range(TILES // 2):
        cross = cross + fast_dot(panels[r], block(PANEL, TRAIL, r), NT)
    cross_x[...] = quadrants(cross).reshape(cross_x.shape)
    phase_one(cross_x, cross_land, 3)

    scale = math.sqrt(run_total)

    def transpose(r, carry):
        rows = pl.ds(pl.multiple_of(r * 128, 128), 128)
        base = pl.multiple_of(r * PITCH, 8)
        high, low = split(columns[pl.ds(base, PANEL), :].T)
        panel_t[rows, :] = jnp.concatenate([high, low], axis=1)
        trail_t[rows, :] = columns[pl.ds(base + PANEL, TRAIL), :].T * scale
        return carry

    phase_two(gram_x, gram_land, gram_z, 0)
    phase_two(cross_x, cross_land, cross_z, 3)
    lax.fori_loop(0, TILES, transpose, 0)
    phase_three(gram_land, gram_z, gram_all, 0)
    phase_three(cross_land, cross_z, cross_all, 3)

    wait(gram_land, recv_sem.at[2])
    cholesky(gram_all.reshape(PANEL, PANEL), upper_out, inverse, rows_v)
    wait(cross_land, recv_sem.at[5])
    inv_high, inv_low = split(inverse[...])
    high, low = split(cross_all[...].reshape(PANEL, TRAIL))
    coupling = fast_dot(inv_high, high, NN) + (fast_dot(inv_high, low, NN) + fast_dot(inv_low, high, NN))
    coupling_out[...] = coupling
    high, low = split(coupling)
    weights = fast_dot(inv_high, high, TN) + (fast_dot(inv_high, low, TN) + fast_dot(inv_low, high, TN))
    weights_out[...] = weights * -scale
    for k in others:
        wait(panel_degs.at[y], deg_send.at[k - 1])
    for i in range(3):
        wait(gram_land, send_sem.at[i])
        wait(cross_land, send_sem.at[i + 3])


def update_kernel(upper_ref, coupling_ref, weights_ref, trail_t, panel_t, upper_out, coupling_out, updated_out, buf, sem):
    small = [
        pltpu.make_async_copy(upper_ref, upper_out, sem.at[0]),
        pltpu.make_async_copy(coupling_ref, coupling_out, sem.at[1]),
    ]
    for copy in small:
        copy.start()
    high, low = split(weights_ref[...])
    stacked = jnp.concatenate([high, high, low], axis=0)
    part = 2048 // 16
    large = []
    for p in range(16):
        rows = pl.ds(p * part, part)
        panel = panel_t[rows, :]
        panel = jnp.concatenate([panel, panel[:, :PANEL]], axis=1)
        buf[rows, :] = trail_t[rows, :] + fast_dot(panel, stacked, NN)
        large.append(pltpu.make_async_copy(buf.at[rows, :], updated_out.at[rows, :], sem.at[2 + p]))
        large[-1].start()
    for copy in small + large:
        copy.wait()


def shards(points, run_weights, panel_degrees, trailing_degrees):
    run_total = float(points.shape[1] * lax.axis_size("sample"))
    f32, i32 = jnp.float32, jnp.int32
    vmem, hbm = pl.BlockSpec(memory_space=pltpu.VMEM), pl.BlockSpec(memory_space=pltpu.HBM)
    dma = pltpu.SemaphoreType.DMA
    chunk, wide = (16, PANEL), (16, TRAIL)
    upper = jax.ShapeDtypeStruct((PANEL, PANEL), f32)
    coupling = jax.ShapeDtypeStruct((PANEL, TRAIL), f32)
    updated = jax.ShapeDtypeStruct((2048, TRAIL), f32)
    parts = pl.pallas_call(
        functools.partial(kernel, run_total),
        out_shape=[upper, coupling, coupling, updated, jax.ShapeDtypeStruct((2048, 2 * PANEL), jnp.bfloat16)],
        in_specs=[hbm] * 4,
        out_specs=[vmem] * 5,
        scratch_shapes=[
            pltpu.VMEM((10, 2048), f32),
            pltpu.VMEM((TILES, 128), f32),
            pltpu.VMEM((10, TRAIL), i32),
            pltpu.VMEM((10, TILES, 128), f32),
            pltpu.VMEM((343, TILES, 128), f32),
            pltpu.VMEM((343, TILES, 128), f32),
            pltpu.VMEM((49, TILES, 128), f32),
            pltpu.VMEM((49, TILES, 128), f32),
            pltpu.VMEM((TILES * PITCH, 128), f32),
            pltpu.VMEM((4, TRAIL), i32),
            pltpu.SMEM((4, TRAIL), i32),
            pltpu.SMEM((RING, 10, 16), i32),
            pltpu.VMEM((RING,) + chunk, f32),
            pltpu.VMEM((RING - 1,) + chunk, f32),
            pltpu.VMEM((RING,) + chunk, f32),
            pltpu.VMEM((RING,) + chunk, f32),
            pltpu.VMEM((RING,) + wide, f32),
            pltpu.VMEM((RING - 1,) + wide, f32),
            pltpu.VMEM((RING,) + wide, f32),
            pltpu.VMEM((RING,) + wide, f32),
            pltpu.VMEM((PANEL, PANEL), f32),
            pltpu.VMEM((72, 128), f32),
            dma((4,)),
            dma,
            dma((RING - 1,)),
            dma((RING - 1,)),
            dma((6,)),
            dma((6,)),
        ],
        name="panel_step",
        compiler_params=pltpu.CompilerParams(
            collective_id=0, has_side_effects=True, vmem_limit_bytes=32 * 2**20
        ),
    )(*(pltpu.with_memory_space_constraint(a, pltpu.HBM) for a in (
        points, run_weights.reshape(TILES, 128), panel_degrees, trailing_degrees
    )))
    return pl.pallas_call(
        update_kernel,
        out_shape=[upper, coupling, updated],
        in_specs=[vmem] * 5,
        out_specs=[hbm] * 3,
        scratch_shapes=[pltpu.VMEM((2048, TRAIL), f32), dma((18,))],
        name="update_step",
        compiler_params=pltpu.CompilerParams(vmem_limit_bytes=16 * 2**20),
    )(*parts)


def solution(mesh):
    in_specs = (P(None, "sample"), P("sample"), P(None, "basis"), P(None, "basis"))
    out_specs = (P(), P(None, "basis"), P("sample", "basis"))
    return jax.shard_map(shards, mesh=mesh, in_specs=in_specs, out_specs=out_specs, check_vma=False)
```

```python
import functools
import math

import jax
import jax.numpy as jnp
from jax import lax
from jax.experimental import pallas as pl
from jax.experimental.pallas import tpu as pltpu
from jax.sharding import PartitionSpec as P

DEG = 6
LEVELS = DEG + 1
TILES = 16
PANEL = 128
TRAIL = 256
COLS = PANEL + TRAIL
PITCH = COLS + 8
FAR_FIRST = (4, 3, 5, 2, 6, 1, 7)
RING = 8
MESH = pl.DeviceIdType.MESH
NN = (((1,), (0,)), ((), ()))
NT = (((1,), (1,)), ((), ()))
TN = (((0,), (0,)), ((), ()))


def lane_splat(row, lane):
    return jnp.broadcast_to(row[:, lane:lane + 1], (8, 128))


def cholesky(gram_ref, upper_ref, inverse_ref, rows_ref):
    sub = lax.broadcasted_iota(jnp.int32, (8, 128), 0)
    lane = lax.broadcasted_iota(jnp.int32, (8, 128), 1)
    rows = [gram_ref[8 * i:8 * i + 8, :] for i in range(16)]

    def all_sublanes(row):
        return jnp.broadcast_to(rows_ref[row:row + 1, :], (8, 128))

    for k in range(16):
        first, last = 8 * k, k == 15
        mid = (lane >= first) & (lane < first + 8)
        for j in range(8):
            rows_ref[8 * j:8 * j + 8, :] = lane_splat(rows[k], first + j)
        rows_ref[64:72, :] = rows[k]
        diag = [[all_sublanes(8 * j + i) if i >= j else None for j in range(8)] for i in range(8)]
        up = [all_sublanes(64 + j) for j in range(8)]
        lo = [jnp.where(mid, jnp.where(lane == first + j, 1.0, 0.0), up[j]) for j in range(8)]
        following = None if last else [lane_splat(rows[k + 1], first + j) for j in range(8)]
        low = [[None] * 8 for _ in range(8)]
        inv = [None] * 8
        change = None
        for j in range(8):
            inv[j] = lax.rsqrt(diag[j][j])
            up[j] = up[j] * inv[j]
            lo[j] = lo[j] * inv[j]
            for i in range(j + 1, 8):
                low[i][j] = diag[i][j] * inv[j]
            if not last:
                following[j] = following[j] * inv[j]
                term = following[j] * lo[j]
                change = term if change is None else change + term
            for i in range(j + 1, 8):
                for m in range(i, 8):
                    diag[m][i] = diag[m][i] - low[m][j] * low[i][j]
                up[i] = up[i] - low[i][j] * up[j]
                lo[i] = lo[i] - low[i][j] * lo[j]
                if not last:
                    following[i] = following[i] - low[i][j] * following[j]
        up_rows, lo_rows = up[0], lo[0]
        for j in range(1, 8):
            up_rows = jnp.where(sub == j, up[j], up_rows)
            lo_rows = jnp.where(sub == j, lo[j], lo_rows)
        upper_ref[first:first + 8, :] = jnp.where(lane >= sub + first, up_rows, 0.0)
        inverse_ref[first:first + 8, :] = jnp.where(lane < first + 8, lo_rows, 0.0)
        if last:
            break
        rows[k + 1] = jnp.where(mid, 0.0, rows[k + 1]) - change
        if k == 14:
            continue
        for j in reversed(range(8)):
            lo[j] = lo[j] * inv[j]
            for i in range(j):
                lo[i] = lo[i] - low[j][i] * lo[j]
        for i in range(k + 2, 16):
            kept = jnp.where(mid, 0.0, rows[i])
            for j in range(8):
                kept = kept - lane_splat(rows[i], first + j) * lo[j]
            rows[i] = kept


def legendre(coord):
    values = [jnp.ones_like(coord), coord]
    for k in range(1, DEG):
        values.append(((2.0 * k + 1.0) * coord * values[k] - k * values[k - 1]) * (1.0 / (k + 1.0)))
    return [values[k] * math.sqrt(2.0 * k + 1.0) for k in range(LEVELS)]


def fill_tables(coords_ref, weight, triples, pairs):
    for group, table in enumerate(triples):
        first, second, third = (legendre(coords_ref[3 * group + d]) for d in range(3))
        for a in range(LEVELS):
            for b in range(LEVELS - a):
                head = first[a] * second[b]
                for c in range(LEVELS - a - b):
                    table[a * 49 + b * 7 + c] = head * third[c]
    for group, table in enumerate(pairs):
        first, second = (legendre(coords_ref[6 + 2 * group + d]) for d in range(2))
        if group == 0:
            first = [value * weight for value in first]
        for a in range(LEVELS):
            for b in range(LEVELS - a):
                table[a * 7 + b] = first[a] * second[b]


def table_rows(degree):
    return [
        degree(0) * 49 + degree(1) * 7 + degree(2),
        degree(3) * 49 + degree(4) * 7 + degree(5),
        degree(6) * 7 + degree(7),
        degree(8) * 7 + degree(9),
    ]


def split(value):
    high = value.astype(jnp.bfloat16)
    return high, (value - high.astype(jnp.float32)).astype(jnp.bfloat16)


def fast_dot(left, right, dims):
    return lax.dot_general(left, right, dims, preferred_element_type=jnp.float32)


def kernel(run_total, points_ref, weights_ref, panel_deg_ref, trail_deg_ref,
           upper_out, coupling_out, weights_out, trail_t, panel_t,
           points_v, weights_v, trail_deg_v,
           coords, triple_a, triple_b, pair_a, pair_b, columns,
           trail_idx_v, trail_idx, panel_degs,
           gram_x, gram_land, gram_z, gram_all, cross_x, cross_land, cross_z, cross_all,
           inverse, rows_v, trail_halves, in_sem, local_sem, deg_send, deg_recv, send_sem, recv_sem):
    s, y = lax.axis_index("sample"), lax.axis_index("basis")
    z, q = s // RING, lax.rem(s, RING)
    others = range(1, RING)
    y_peers = [(s, lax.rem(y + k, RING)) for k in others]
    q_peers = [(z * RING + lax.rem(q + k, RING), y) for k in others]
    z_peers = [(lax.rem(z + k, RING) * RING + q, y) for k in others]

    barrier = pltpu.get_barrier_semaphore()
    for k in FAR_FIRST:
        for peers in (y_peers, z_peers, q_peers):
            pl.semaphore_signal(barrier, inc=1, device_id=peers[k - 1], device_id_type=MESH)
    loads = [
        pltpu.make_async_copy(src, dst, in_sem.at[i])
        for i, (src, dst) in enumerate([
            (panel_deg_ref, panel_degs.at[y]), (trail_deg_ref, trail_deg_v), (points_ref, points_v), (weights_ref, weights_v)
        ])
    ]
    for load in loads:
        load.start()

    def send(src, dst, ssem, rsem, peer):
        pltpu.make_async_remote_copy(
            src_ref=src, dst_ref=dst, send_sem=ssem, recv_sem=rsem, device_id=peer, device_id_type=MESH
        ).start()

    def wait(ref, sem):
        pltpu.make_async_copy(ref, ref, sem).wait()

    away = jnp.minimum(y, RING - y)

    def exchange_degrees(now):
        @pl.when(now)
        def _():
            loads[0].wait()
            pl.semaphore_wait(barrier, 3 * (RING - 1))
            for k in FAR_FIRST:
                send(panel_degs.at[y], panel_degs.at[y], deg_send.at[k - 1], deg_recv.at[k - 1], y_peers[k - 1])

    exchange_degrees(away >= 3)

    loads[1].wait()
    for g, row in enumerate(table_rows(lambda d: trail_deg_v[d:d + 1, :])):
        trail_idx_v[g:g + 1, :] = row
    idx_copy = pltpu.make_async_copy(trail_idx_v, trail_idx, local_sem)
    idx_copy.start()
    loads[2].wait()
    loads[3].wait()
    for r in range(TILES):
        coords[:, r, :] = points_v[:, 128 * r:128 * r + 128]
    weight = jnp.sqrt(weights_v[...] / run_total)
    fill_tables(coords, weight, (triple_a, triple_b), (pair_a, pair_b))
    exchange_degrees(jnp.logical_and(away > 0, away < 3))
    idx_copy.wait()

    def product(i, j, k, m):
        return triple_a[i] * triple_b[j] * (pair_a[k] * pair_b[m])

    def trail_column(j, carry):
        value = product(trail_idx[0, j], trail_idx[1, j], trail_idx[2, j], trail_idx[3, j])
        columns[pl.ds(PANEL + j, TILES, stride=PITCH), :] = value
        return carry

    lax.fori_loop(0, TRAIL, trail_column, 0, unroll=8)
    exchange_degrees(away == 0)

    def panel_block(owner):
        def panel_column(i, carry):
            rows = table_rows(lambda d: panel_degs[owner, d, i])
            columns[pl.ds(owner * 16 + i, TILES, stride=PITCH), :] = product(*rows)
            return carry

        lax.fori_loop(0, 16, panel_column, 0, unroll=4)

    def block(start, size, r):
        high, low = split(jnp.concatenate(
            [columns[pl.ds((2 * r + h) * PITCH + start, size), :] for h in range(2)], axis=1
        ))
        return jnp.concatenate([high, low], axis=0)

    for r in range(TILES // 2):
        trail_halves[r] = block(PANEL, TRAIL, r)

    panel_block(y)
    for k in (1, 7, 2, 6, 3, 5, 4):
        owner = lax.rem(y + RING - k, RING)
        wait(panel_degs.at[owner], deg_recv.at[k - 1])
        panel_block(owner)

    def quadrants(total):
        rows, cols = total.shape[0] // 2, total.shape[1] // 2
        return (total[rows:, cols:] + (total[:rows, cols:] + total[rows:, :cols])) + total[:rows, :cols]

    def phase_one(x, land, i):
        for k in FAR_FIRST:
            send(x.at[lax.rem(q + k, RING)], land.at[k - 1], send_sem.at[i], recv_sem.at[i], q_peers[k - 1])

    def phase_two(x, land, all_z, i):
        wait(land, recv_sem.at[i])
        part = x[q]
        for k in range(RING - 1):
            part = part + land[k]
        all_z[z] = part
        for k in FAR_FIRST:
            send(all_z.at[z], all_z.at[z], send_sem.at[i + 1], recv_sem.at[i + 1], z_peers[k - 1])

    def phase_three(land, all_z, out, i):
        wait(land, recv_sem.at[i + 1])
        total = all_z[0]
        for k in others:
            total = total + all_z[k]
        out[q] = total
        for k in FAR_FIRST:
            send(out.at[q], out.at[q], send_sem.at[i + 2], recv_sem.at[i + 2], q_peers[k - 1])

    panels = [block(0, PANEL, r) for r in range(TILES // 2)]
    gram = fast_dot(panels[0], panels[0], NT)
    for r in range(1, TILES // 2):
        gram = gram + fast_dot(panels[r], panels[r], NT)
    gram_x[...] = quadrants(gram).reshape(gram_x.shape)
    phase_one(gram_x, gram_land, 0)
    cross = jnp.zeros((2 * PANEL, 2 * TRAIL), jnp.float32)
    for r in range(TILES // 2):
        cross = cross + fast_dot(panels[r], trail_halves[r], NT)
    cross_x[...] = quadrants(cross).reshape(cross_x.shape)
    phase_one(cross_x, cross_land, 3)

    scale = math.sqrt(run_total)

    def transpose(r, carry):
        rows = pl.ds(pl.multiple_of(r * 128, 128), 128)
        base = pl.multiple_of(r * PITCH, 8)
        high, low = split(columns[pl.ds(base, PANEL), :].T)
        panel_t[rows, :] = jnp.concatenate([high, low], axis=1)
        trail_t[rows, :] = columns[pl.ds(base + PANEL, TRAIL), :].T * scale
        return carry

    phase_two(gram_x, gram_land, gram_z, 0)
    phase_two(cross_x, cross_land, cross_z, 3)
    lax.fori_loop(0, TILES, transpose, 0)
    phase_three(gram_land, gram_z, gram_all, 0)
    phase_three(cross_land, cross_z, cross_all, 3)

    wait(gram_land, recv_sem.at[2])
    cholesky(gram_all.reshape(PANEL, PANEL), upper_out, inverse, rows_v)
    wait(cross_land, recv_sem.at[5])
    inv_high, inv_low = split(inverse[...])
    high, low = split(cross_all[...].reshape(PANEL, TRAIL))
    coupling = fast_dot(inv_high, high, NN) + (fast_dot(inv_high, low, NN) + fast_dot(inv_low, high, NN))
    coupling_out[...] = coupling
    high, low = split(coupling)
    weights = fast_dot(inv_high, high, TN) + (fast_dot(inv_high, low, TN) + fast_dot(inv_low, high, TN))
    weights_out[...] = weights * -scale
    for k in others:
        wait(panel_degs.at[y], deg_send.at[k - 1])
    for i in range(3):
        wait(gram_land, send_sem.at[i])
        wait(cross_land, send_sem.at[i + 3])


def update_kernel(upper_ref, coupling_ref, weights_ref, trail_t, panel_t, upper_out, coupling_out, updated_out, buf, sem):
    small = [
        pltpu.make_async_copy(upper_ref, upper_out, sem.at[0]),
        pltpu.make_async_copy(coupling_ref, coupling_out, sem.at[1]),
    ]
    for copy in small:
        copy.start()
    high, low = split(weights_ref[...])
    stacked = jnp.concatenate([high, high, low], axis=0)
    part = 2048 // 16
    large = []
    for p in range(16):
        rows = pl.ds(p * part, part)
        panel = panel_t[rows, :]
        panel = jnp.concatenate([panel, panel[:, :PANEL]], axis=1)
        buf[rows, :] = trail_t[rows, :] + fast_dot(panel, stacked, NN)
        large.append(pltpu.make_async_copy(buf.at[rows, :], updated_out.at[rows, :], sem.at[2 + p]))
        large[-1].start()
    for copy in small + large:
        copy.wait()


def shards(points, run_weights, panel_degrees, trailing_degrees):
    run_total = float(points.shape[1] * lax.axis_size("sample"))
    f32, i32 = jnp.float32, jnp.int32
    vmem, hbm = pl.BlockSpec(memory_space=pltpu.VMEM), pl.BlockSpec(memory_space=pltpu.HBM)
    dma = pltpu.SemaphoreType.DMA
    chunk, wide = (16, PANEL), (16, TRAIL)
    upper = jax.ShapeDtypeStruct((PANEL, PANEL), f32)
    coupling = jax.ShapeDtypeStruct((PANEL, TRAIL), f32)
    updated = jax.ShapeDtypeStruct((2048, TRAIL), f32)
    parts = pl.pallas_call(
        functools.partial(kernel, run_total),
        out_shape=[upper, coupling, coupling, updated, jax.ShapeDtypeStruct((2048, 2 * PANEL), jnp.bfloat16)],
        in_specs=[hbm] * 4,
        out_specs=[vmem] * 5,
        scratch_shapes=[
            pltpu.VMEM((10, 2048), f32),
            pltpu.VMEM((TILES, 128), f32),
            pltpu.VMEM((10, TRAIL), i32),
            pltpu.VMEM((10, TILES, 128), f32),
            pltpu.VMEM((343, TILES, 128), f32),
            pltpu.VMEM((343, TILES, 128), f32),
            pltpu.VMEM((49, TILES, 128), f32),
            pltpu.VMEM((49, TILES, 128), f32),
            pltpu.VMEM((TILES * PITCH, 128), f32),
            pltpu.VMEM((4, TRAIL), i32),
            pltpu.SMEM((4, TRAIL), i32),
            pltpu.SMEM((RING, 10, 16), i32),
            pltpu.VMEM((RING,) + chunk, f32),
            pltpu.VMEM((RING - 1,) + chunk, f32),
            pltpu.VMEM((RING,) + chunk, f32),
            pltpu.VMEM((RING,) + chunk, f32),
            pltpu.VMEM((RING,) + wide, f32),
            pltpu.VMEM((RING - 1,) + wide, f32),
            pltpu.VMEM((RING,) + wide, f32),
            pltpu.VMEM((RING,) + wide, f32),
            pltpu.VMEM((PANEL, PANEL), f32),
            pltpu.VMEM((72, 128), f32),
            pltpu.VMEM((TILES // 2, 2 * TRAIL, 256), jnp.bfloat16),
            dma((4,)),
            dma,
            dma((RING - 1,)),
            dma((RING - 1,)),
            dma((6,)),
            dma((6,)),
        ],
        name="panel_step",
        compiler_params=pltpu.CompilerParams(
            collective_id=0, has_side_effects=True, vmem_limit_bytes=32 * 2**20
        ),
    )(*(pltpu.with_memory_space_constraint(a, pltpu.HBM) for a in (
        points, run_weights.reshape(TILES, 128), panel_degrees, trailing_degrees
    )))
    return pl.pallas_call(
        update_kernel,
        out_shape=[upper, coupling, updated],
        in_specs=[vmem] * 5,
        out_specs=[hbm] * 3,
        scratch_shapes=[pltpu.VMEM((2048, TRAIL), f32), dma((18,))],
        name="update_step",
        compiler_params=pltpu.CompilerParams(vmem_limit_bytes=16 * 2**20),
    )(*parts)


def solution(mesh):
    in_specs = (P(None, "sample"), P("sample"), P(None, "basis"), P(None, "basis"))
    out_specs = (P(), P(None, "basis"), P("sample", "basis"))
    return jax.shard_map(shards, mesh=mesh, in_specs=in_specs, out_specs=out_specs, check_vma=False)
```
